128 devices in a mesh: dp: 16 (over y_hi, x, core), tensor: 8 (over z, y_lo).
Axes of the slice: x: 4, y: 4 (y_hi: 2, y_lo: 2; y = y_hi * 2 + y_lo), z: 4, core: 2. Of those that a mesh axis runs over, the one named last changes fastest.
Arguments:
- out_grad: bfloat16 [8192, 4096], P(('dp', 'tensor')), may hold values from -24 to 24
- hidden_act: bfloat16 [8192, 14336], P('dp', 'tensor'), may hold values from -6 to 6
- w_down: bfloat16 [4096, 14336], P(None, 'tensor'), may hold values from -0.09375 to 0.09375
Outputs:
- hidden_grad: bfloat16 [8192, 14336], P('dp', 'tensor')
- weight_grad: bfloat16 [4096, 14336], P('dp', 'tensor')
- factor: float32 [4096, 4096], P('dp', 'tensor')
The draws below stay inside these ranges and needn't reach their ends.
All inputs are finite; a program needn't handle non-finite values.
Results may differ from the reference program's by a relative error of at most 0.02.
Values may be sent and summed in bfloat16 or wider, within the bound.
A program may use at most 128 MiB of HBM per device.

```python
import math
import jax
import jax.numpy as jnp
from jax import lax

D = 4096
FF = 14336
TOK_DP = 512
TOKENS = 8192


def spiked(array, stream_key, source, target, blocks, factor):
    def block_of(dim):
        return (jnp.arange(array.shape[dim]) // (array.shape[dim] // blocks)).reshape((-1,) + (1,) * (array.ndim - 1 - dim))

    near = jax.random.permutation(stream_key, blocks)[block_of(target)]
    second = (block_of(target) + blocks // 2) % blocks
    return jnp.where((block_of(source) == near) | (block_of(source) == second), factor * array, array)


def steps_of(rng, dims, cuts, least, top_value):
    gain = 1.0
    for axis_at, blocks in cuts:
        draws = jax.random.uniform(jax.random.fold_in(jax.random.fold_in(rng, 6), axis_at), (blocks,), jnp.float32, least / len(cuts), top_value / len(cuts))
        gain = gain * jnp.repeat(jnp.exp(draws), dims[axis_at] // blocks).reshape((-1,) + (1,) * (len(dims) - 1 - axis_at))
    return gain


def gaussian(stream_key, extent, spread, most, pieces=(), kind=jnp.bfloat16):
    gain = steps_of(stream_key, extent, pieces, -0.22, 0.18) if pieces else 1.0
    drawn = jax.random.normal(stream_key, extent, jnp.float32) * spread * gain
    return jnp.minimum(jnp.maximum(drawn, -most), most).astype(kind)


def gaussian_with(stream_key, shape, width, reach, cuts, heavy, kind=jnp.bfloat16):
    drawn = width * jax.random.normal(stream_key, shape, jnp.float32)
    if cuts:
        drawn = drawn * steps_of(stream_key, shape, cuts, -0.22, 0.18)
    return jnp.clip(spiked(drawn, jax.random.fold_in(stream_key, 3), *heavy), -reach, reach).astype(kind)


def setup_inputs(seed: int = 0) -> dict:
    key_of = jax.random.split(jax.random.key(seed), 4)
    return {
        "out_grad": gaussian_with(key_of[0], (TOKENS, D), 1.0, 24.0, ((0, 128),), (0, 1, 128, 5.5)),
        "hidden_act": gaussian(key_of[1], (TOKENS, FF), 1.0, 6.0, ((0, 16), (1, 8))),
        "w_down": gaussian(key_of[2], (D, FF), D ** -0.5, 0.09375, ((1, 8),)),
    }


def reference(out_grad, hidden_act, w_down):
    hidden_grad = jnp.dot(out_grad, w_down, preferred_element_type=jnp.float32).astype(jnp.bfloat16)
    scale = 1.0 / math.sqrt(TOKENS)

    def batch_step(carry, index):
        start = (index * TOK_DP).astype(jnp.int32)
        rows_grad = lax.dynamic_slice_in_dim(out_grad, start, TOK_DP, 0)
        rows_act = lax.dynamic_slice_in_dim(hidden_act, start, TOK_DP, 0)
        term = lax.dot_general(rows_grad, rows_act, (((0,), (0,)), ((), ())), preferred_element_type=jnp.float32) * scale
        rounded = lax.optimization_barrier(term.astype(jnp.bfloat16))
        return (carry + rounded.astype(jnp.float32), None)
    start_sum = jnp.zeros((D, FF), jnp.float32)
    summed, _ = lax.scan(batch_step, start_sum, jnp.arange(TOKENS // TOK_DP, dtype=jnp.int32))
    weight_grad = summed.astype(jnp.bfloat16)
    factor = lax.dot_general(out_grad, out_grad, (((0,), (0,)), ((), ())), preferred_element_type=jnp.float32) / TOKENS
    return (hidden_grad, weight_grad, factor)
```

```python
import math

import jax
import jax.numpy as jnp
from jax import lax
from jax.experimental import pallas as pl
from jax.experimental.pallas import tpu as pltpu
from jax.sharding import PartitionSpec as P

MESH = pl.DeviceIdType.MESH
BF16 = jnp.bfloat16
F32 = jnp.float32

ORDER = ((1, 2), (1, 1), (1, 3), (0, 2), (0, 1), (0, 3), (1, 0), (0, 0))
SLOT = {pair: slot for slot, pair in enumerate(ORDER)}
CHIPS = len(ORDER)
TILE = 256
FIRST_X = 1024
COPIES = 96


def kernel(own_grad, own_act, weight, hidden_out, wgrad_out, factor_out,
           grad, grad_sib, grad_cols, act, w, left, part_w, part_f, hidden, wgrad, factor, boxes, send_sem, recv_sem, local_sem):
    rows, width = own_grad.shape
    tokens, units = own_act.shape
    tensor = tokens // rows
    chunk = width // CHIPS
    share = chunk // 2
    half = share // 2
    dp, t = lax.axis_index("dp"), lax.axis_index("tensor")
    core, x, y = dp % 2, (dp // 2) % 4, dp // 8
    z, y_lo = t // 2, t % 2

    def on_x(step):
        return (y * 8 + ((x + step) % 4) * 2 + core, t)

    def on_z(step):
        return (dp, ((z + step) % 4) * 2 + y_lo)

    sibling = (dp + 1 - 2 * core, t)
    right, left_chip = on_x(1), on_x(3)
    across = ((1 - y) * 8 + x * 2 + core, t)
    partner = (dp, z * 2 + 1 - y_lo)
    near_z = (on_z(1), on_z(3), on_z(2))

    barrier = pltpu.get_barrier_semaphore()
    everyone = (sibling, right, left_chip, across, partner) + near_z
    for device in everyone:
        pl.semaphore_signal(barrier, inc=1, device_id=device, device_id_type=MESH)

    remotes, locals_ = [], []

    def send(src, dst, device):
        number = len(remotes)
        copy = pltpu.make_async_remote_copy(
            src_ref=src, dst_ref=dst, send_sem=send_sem.at[number], recv_sem=recv_sem.at[number],
            device_id=device, device_id_type=MESH)
        copy.start()
        remotes.append(copy)
        return copy

    def move(src, dst):
        copy = pltpu.make_async_copy(src, dst, local_sem.at[len(locals_)])
        copy.start()
        locals_.append(copy)
        return copy

    def first_col(slot):
        dy, dx = ORDER[slot]
        return (((y + dy) % 2) * 4 + (x + dx) % 4) * chunk

    def columns(slot):
        return pl.ds(pl.multiple_of(first_col(slot), chunk), chunk)

    def share_of(slot, which):
        return pl.ds(pl.multiple_of(first_col(slot) + which * share, share), share)

    own_rows = pl.ds(pl.multiple_of(t * rows, rows), rows)
    pair_rows = pl.ds(pl.multiple_of(z * 2 * rows, 2 * rows), 2 * rows)

    own_here = move(own_grad, grad.at[own_rows, :])
    act_here = move(own_act, act.at[pl.ds(0, tokens)])
    pl.semaphore_wait(barrier, len(everyone))

    from_partner = [send(own_grad.at[:, columns(s)], grad.at[own_rows, columns(s)], partner) for s in range(CHIPS)]
    act_there = send(own_act, act.at[pl.ds(tokens, tokens)], sibling)
    w_here = move(weight, w)
    along_z, to_sibling = {}, {}

    def gather_z(slot):
        from_partner[slot].wait_recv()
        piece = grad.at[pair_rows, columns(slot)]
        along_z[slot] = [send(piece, piece, device) for device in near_z]

    def gather_sibling(slot):
        for copy in along_z[slot]:
            copy.wait_recv()
        to_sibling[slot] = send(grad.at[:, share_of(slot, 1 - core)], grad_sib.at[slot], sibling)

    class Columns:
        def __init__(self, part, start, count, x_first, box):
            self.part, self.cols, self.x_first = part, pl.ds(start, count), x_first
            self.relay_l, self.relay_r, self.end_l, self.end_r, self.box_y = box
            self.relays, self.ends, self.over_y = {}, {}, {}

        def at(self, dy, dx, low=0, count=share):
            return self.part.at[SLOT[dy, dx], pl.ds(low, count), self.cols]

        def far(self, dy):
            self.relays[dy] = (
                send(self.at(dy, 2, 0, half), self.relay_l.at[dy], right),
                send(self.at(dy, 2, half, half), self.relay_r.at[dy], left_chip))

        def near_right(self, dy):
            self.ends[dy, 1, 1] = send(self.at(dy, 1, half, half), self.end_l.at[dy, pl.ds(half, half)], right)

        def near_left(self, dy):
            self.ends[dy, 3, 0] = send(self.at(dy, 3, 0, half), self.end_r.at[dy, pl.ds(0, half)], left_chip)

        def relay_right(self, dy):
            self.relays[dy][0].wait_recv()
            mine = self.at(dy, 1, 0, half)
            mine[...] = (mine[...].astype(F32) + self.relay_l[dy].astype(F32)).astype(BF16)
            self.ends[dy, 1, 0] = send(mine, self.end_l.at[dy, pl.ds(0, half)], right)

        def relay_left(self, dy):
            self.relays[dy][1].wait_recv()
            mine = self.at(dy, 3, half, half)
            mine[...] = (mine[...].astype(F32) + self.relay_r[dy].astype(F32)).astype(BF16)
            self.ends[dy, 3, 1] = send(mine, self.end_r.at[dy, pl.ds(half, half)], left_chip)

        def x_sum(self, dy):
            for place in ((1, 0), (1, 1), (3, 0), (3, 1)):
                self.ends[(dy,) + place].wait_recv()
            return self.at(dy, 0)[...].astype(F32) + self.end_l[dy].astype(F32) + self.end_r[dy].astype(F32)

        def send_y(self, dx):
            self.over_y[dx] = send(self.at(1, dx), self.box_y.at[dx], across)

        def add_y(self, dx):
            self.over_y[dx].wait_recv()
            mine = self.at(0, dx)
            mine[...] = (mine[...].astype(F32) + self.box_y[dx].astype(F32)).astype(BF16)

        def end_y(self):
            self.at(1, 0)[...] = self.x_sum(1).astype(BF16)
            self.over_y[0] = send(self.at(1, 0), self.box_y, across)

        def total(self):
            value = self.x_sum(0)
            if self.x_first:
                self.over_y[0].wait_recv()
                value = value + self.box_y[...].astype(F32)
            return value

    wx = Columns(part_w, 0, FIRST_X, True, boxes[0:5])
    wy = Columns(part_w, FIRST_X, units - FIRST_X, False, boxes[5:10])
    fx = Columns(part_f, 0, chunk, True, boxes[10:15])

    def multiply(slot):
        to_sibling[slot].wait_recv()
        left[slot, :, pl.ds(0, tokens)] = grad[:, share_of(slot, core)].T
        left[slot, :, pl.ds(tokens, tokens)] = grad_sib[slot].T

        @pl.loop(0, units // TILE)
        def _(n):
            cols = pl.ds(pl.multiple_of(n * TILE, TILE), TILE)
            part_w[slot, :, cols] = jnp.dot(left[slot], act[:, cols], preferred_element_type=F32).astype(BF16)

    def multiply_factor(slot):
        own = left[slot, :, pl.ds(0, tokens)]
        other = left[slot, :, pl.ds(tokens, tokens)]
        cols = pl.ds(pl.multiple_of(t * chunk, chunk), chunk)
        value = jnp.dot(own, grad[:, cols], preferred_element_type=F32)
        value = value + jnp.dot(other, grad_cols[...], preferred_element_type=F32)
        part_f[slot] = value.astype(BF16)

    def multiply_hidden(first, last):
        @pl.loop(first, last)
        def _(n):
            cols = pl.ds(pl.multiple_of(n * TILE, TILE), TILE)
            hidden[:, cols] = jnp.dot(grad[...], w[:, cols], preferred_element_type=F32).astype(BF16)

    own_here.wait()
    gather_z(0)
    gather_z(1)
    gather_sibling(0)
    act_here.wait()
    act_there.wait_recv()
    for slot, (dy, dx) in enumerate(ORDER):
        multiply(slot)
        if dx == 2:
            wx.far(dy)
        if dx == 1:
            wx.near_right(dy)
        if dx == 3:
            wx.near_left(dy)
        if dy == 1:
            wy.send_y(dx)
        if slot + 2 < CHIPS:
            gather_z(slot + 2)
        if dx == 1:
            wx.relay_right(dy)
        if dx == 3:
            wx.relay_left(dy)
        if slot + 1 < CHIPS:
            gather_sibling(slot + 1)
        else:
            cols = pl.ds(pl.multiple_of(t * chunk, chunk), chunk)
            to_sibling["cols"] = send(grad.at[:, cols], grad_cols, sibling)
        if dy == 0 and dx != 0:
            wy.add_y(dx)
            if dx == 2:
                wy.far(0)
            if dx == 1:
                wy.near_right(0)
                wy.relay_right(0)
            if dx == 3:
                wy.near_left(0)
                wy.relay_left(0)

    to_sibling["cols"].wait_recv()
    for slot, (dy, dx) in enumerate(ORDER):
        multiply_factor(slot)
        if dx == 2:
            fx.far(dy)
        if dx == 1:
            fx.near_right(dy)
        if dx == 3:
            fx.near_left(dy)
    wx.end_y()
    w_here.wait()
    multiply_hidden(0, 2)
    for dy in (1, 0):
        fx.relay_right(dy)
        fx.relay_left(dy)
    multiply_hidden(2, 5)
    fx.end_y()
    multiply_hidden(5, units // TILE)
    hidden_done = move(hidden, hidden_out)

    scale = 1.0 / math.sqrt(tokens * 16)
    wy.add_y(0)
    wgrad[:, wx.cols] = (wx.total() * scale).astype(BF16)
    wgrad[:, wy.cols] = (wy.total() * scale).astype(BF16)
    wgrad_done = move(wgrad, wgrad_out)
    factor[...] = fx.total() / (tokens * 16)
    factor_done = move(factor, factor_out)
    for copy in remotes:
        copy.wait_send()
    for copy in (hidden_done, wgrad_done, factor_done):
        copy.wait()


def shards(out_grad, hidden_act, w_down):
    rows, width = out_grad.shape
    tokens, units = hidden_act.shape
    chunk = width // CHIPS
    share, half = chunk // 2, chunk // 4

    def boxes(count, x_first):
        ways = 2 if x_first else 1
        relay, end = pltpu.VMEM((ways, half, count), BF16), pltpu.VMEM((ways, share, count), BF16)
        over = pltpu.VMEM((share, count) if x_first else (4, share, count), BF16)
        return [relay, relay, end, end, over]

    def body(*refs):
        kernel(*refs[:17], refs[17:32], *refs[32:])

    return pl.pallas_call(
        body,
        out_shape=(
            jax.ShapeDtypeStruct((tokens, units), BF16),
            jax.ShapeDtypeStruct((share, units), BF16),
            jax.ShapeDtypeStruct((share, chunk), F32),
        ),
        in_specs=[pl.BlockSpec(memory_space=pl.ANY)] * 3,
        out_specs=(pl.BlockSpec(memory_space=pl.ANY),) * 3,
        scratch_shapes=[
            pltpu.VMEM((tokens, width), BF16),
            pltpu.VMEM((CHIPS, tokens, share), BF16),
            pltpu.VMEM((tokens, chunk), BF16),
            pltpu.VMEM((2 * tokens, units), BF16),
            pltpu.VMEM((width, units), BF16),
            pltpu.VMEM((CHIPS, share, 2 * tokens), BF16),
            pltpu.VMEM((CHIPS, share, units), BF16),
            pltpu.VMEM((CHIPS, share, chunk), BF16),
            pltpu.VMEM((tokens, units), BF16),
            pltpu.VMEM((share, units), BF16),
            pltpu.VMEM((share, chunk), F32),
            *boxes(FIRST_X, True),
            *boxes(units - FIRST_X, False),
            *boxes(chunk, True),
            pltpu.SemaphoreType.DMA((COPIES,)),
            pltpu.SemaphoreType.DMA((COPIES,)),
            pltpu.SemaphoreType.DMA((8,)),
        ],
        compiler_params=pltpu.CompilerParams(
            collective_id=0, has_side_effects=True, vmem_limit_bytes=60 * 2**20),
    )(out_grad, hidden_act, w_down)


def solution(mesh):
    return jax.shard_map(
        shards,
        mesh=mesh,
        in_specs=(P(("dp", "tensor"), None), P("dp", "tensor"), P(None, "tensor")),
        out_specs=(P("dp", "tensor"), P("dp", "tensor"), P("dp", "tensor")),
        check_vma=False,
    )
```

```python
import math

import jax
import jax.numpy as jnp
from jax import lax
from jax.experimental import pallas as pl
from jax.experimental.pallas import tpu as pltpu
from jax.sharding import PartitionSpec as P

MESH = pl.DeviceIdType.MESH
BF16 = jnp.bfloat16
F32 = jnp.float32

ORDER = ((1, 2), (0, 2), (1, 1), (1, 3), (0, 3), (0, 1), (1, 0), (0, 0))
SLOT = {pair: slot for slot, pair in enumerate(ORDER)}
CHIPS = len(ORDER)
TILE = 256
FIRST_X = 896
COPIES = 128


EARLY = (0,)
PLAN = (
    ("z", 0), ("z", 1), ("z", 2), ("z", 3), ("z", 4), ("sib", 0), ("mul", 0), ("x", "w", 0), ("y", 2), ("z", 5),
    ("sib", 1), ("mul", 1), ("x", "w", 1), ("sib", 2), ("mul", 2), ("x", "w", 2), ("relay", "w", 2), ("y", 1),
    ("z", 6), ("addy", 2), ("x", "v", 1), ("sib", 3), ("mul", 3), ("relay", "w", 3), ("y", 3), ("sib", 4), ("mul", 4),
    ("relay", "w", 4), ("x", "w", 3), ("z", 7), ("cols",), ("sib", 5), ("mul", 5), ("addy", 1), ("relay", "v", 5),
    ("relay", "w", 5), ("x", "w", 5), ("addy", 3), ("relay", "v", 4), ("x", "v", 4), ("sib", 7), ("sib", 6),
    ("hid", 0, 1), ("mul", 6), ("y", 0), ("endy", "w"), ("colsib",), ("fac", 0), ("fac", 6), ("fac", 2), ("fac", 1),
    ("x", "f", 0), ("fac", 5), ("fac", 4), ("x", "f", 5), ("fac", 3), ("x", "f", 3), ("relay", "f", 2),
    ("relay", "f", 3), ("x", "f", 2), ("x", "f", 1), ("x", "f", 4), ("x", "w", 4), ("x", "v", 5), ("hid", 1, 5),
    ("relay", "f", 4), ("endy", "f"), ("hid", 5, 7), ("relay", "f", 5), ("mul", 7), ("fac", 7), ("addy", 0),
    ("fin", "v"), ("fin", "w"), ("fin", "f"),
)


def kernel(own_grad, own_act, weight, hidden_out, wgrad_out, factor_out,
           grad, grad_sib, cols_own, cols_sib, act, w, left, part_w, part_f, hidden, wgrad, factor, boxes,
           send_sem, recv_sem, local_sem, w_sem):
    rows, width = own_grad.shape
    tokens, units = own_act.shape
    chunk = width // CHIPS
    share = chunk // 2
    half = share // 2
    dp, t = lax.axis_index("dp"), lax.axis_index("tensor")
    core, x, y = dp % 2, (dp // 2) % 4, dp // 8
    z, y_lo = t // 2, t % 2

    def on_x(step):
        return (y * 8 + ((x + step) % 4) * 2 + core, t)

    def on_z(step):
        return (dp, ((z + step) % 4) * 2 + y_lo)

    sibling = (dp + 1 - 2 * core, t)
    right, left_chip = on_x(1), on_x(3)
    across = ((1 - y) * 8 + x * 2 + core, t)
    partner = (dp, z * 2 + 1 - y_lo)
    along = (2, 1, 3)

    barrier = pltpu.get_barrier_semaphore()
    everyone = (sibling, right, left_chip, across, partner) + tuple(on_z(step) for step in along)
    for device in everyone:
        pl.semaphore_signal(barrier, inc=1, device_id=device, device_id_type=MESH)

    remotes, locals_ = [], []

    def send(src, dst, device):
        number = len(remotes)
        copy = pltpu.make_async_remote_copy(
            src_ref=src, dst_ref=dst, send_sem=send_sem.at[number], recv_sem=recv_sem.at[number],
            device_id=device, device_id_type=MESH)
        copy.start()
        remotes.append(copy)
        return copy

    def move(src, dst):
        copy = pltpu.make_async_copy(src, dst, local_sem.at[len(locals_)])
        copy.start()
        locals_.append(copy)
        return copy

    def first_col(slot):
        dy, dx = ORDER[slot]
        return (((y + dy) % 2) * 4 + (x + dx) % 4) * chunk

    def columns(slot):
        return pl.ds(pl.multiple_of(first_col(slot), chunk), chunk)

    def share_of(slot, which):
        return pl.ds(pl.multiple_of(first_col(slot) + which * share, share), share)

    def columns_of(there):
        return pl.ds(pl.multiple_of(there * chunk, chunk), chunk)

    own_rows = pl.ds(pl.multiple_of(t * rows, rows), rows)
    partner_rows = pl.ds(pl.multiple_of((z * 2 + 1 - y_lo) * rows, rows), rows)
    pair_rows = pl.ds(pl.multiple_of(z * 2 * rows, 2 * rows), 2 * rows)

    def w_tile(n):
        cols = pl.ds(pl.multiple_of(n * TILE, TILE), TILE)
        return pltpu.make_async_copy(weight.at[:, cols], w.at[n % 2], w_sem.at[n % 2])

    own_here = move(own_grad, grad.at[own_rows, :])
    act_here = move(own_act, act.at[pl.ds(0, tokens)])
    pl.semaphore_wait(barrier, len(everyone))

    from_partner, along_z, to_sibling, cols = {}, {}, {}, {}

    def gather_y(slot):
        piece = columns(slot)
        from_partner[slot] = send(own_grad.at[:, piece], grad.at[own_rows, piece], partner)

    def gather_own(slot):
        piece = columns(slot)
        along_z[slot] = [send(own_grad.at[:, piece], grad.at[own_rows, piece], on_z(step)) for step in along]

    def gather_z(slot):
        from_partner[slot].wait_recv()
        piece = grad.at[partner_rows if slot in EARLY else pair_rows, columns(slot)]
        along_z.setdefault(slot, []).extend([send(piece, piece, on_z(step)) for step in along])

    def gather_sibling(slot):
        for copy in along_z[slot]:
            copy.wait_recv()
        to_sibling[slot] = send(grad.at[:, share_of(slot, 1 - core)], grad_sib.at[slot], sibling)

    def cols_z():
        cols["here"] = move(grad.at[pair_rows, columns_of(t)], cols_own.at[pair_rows, :])
        cols["z"] = [
            send(grad.at[pair_rows, columns_of(((z + step) % 4) * 2 + y_lo)], cols_own.at[pair_rows, :], on_z(step))
            for step in along]

    def cols_sibling():
        cols["here"].wait()
        for copy in cols["z"]:
            copy.wait_recv()
        cols["sibling"] = send(cols_own, cols_sib, sibling)

    class Columns:
        def __init__(self, part, start, count, x_first, box):
            self.part, self.cols, self.x_first = part, pl.ds(start, count), x_first
            self.relay_l, self.relay_r, self.end_l, self.end_r, self.box_y = box
            self.relays, self.ends, self.over_y = {}, {}, {}

        def at(self, dy, dx, low=0, count=share):
            return self.part.at[SLOT[dy, dx], pl.ds(low, count), self.cols]

        def far(self, dy):
            self.relays[dy] = (
                send(self.at(dy, 2, 0, half), self.relay_l.at[dy], right),
                send(self.at(dy, 2, half, half), self.relay_r.at[dy], left_chip))

        def near_right(self, dy):
            self.ends[dy, 1, 1] = send(self.at(dy, 1, half, half), self.end_l.at[dy, pl.ds(half, half)], right)

        def near_left(self, dy):
            self.ends[dy, 3, 0] = send(self.at(dy, 3, 0, half), self.end_r.at[dy, pl.ds(0, half)], left_chip)

        def relay_right(self, dy):
            self.relays[dy][0].wait_recv()
            mine = self.at(dy, 1, 0, half)
            mine[...] = (mine[...].astype(F32) + self.relay_l[dy].astype(F32)).astype(BF16)
            self.ends[dy, 1, 0] = send(mine, self.end_l.at[dy, pl.ds(0, half)], right)

        def relay_left(self, dy):
            self.relays[dy][1].wait_recv()
            mine = self.at(dy, 3, half, half)
            mine[...] = (mine[...].astype(F32) + self.relay_r[dy].astype(F32)).astype(BF16)
            self.ends[dy, 3, 1] = send(mine, self.end_r.at[dy, pl.ds(half, half)], left_chip)

        def x_sum(self, dy):
            for place in ((1, 0), (1, 1), (3, 0), (3, 1)):
                self.ends[(dy,) + place].wait_recv()
            return self.at(dy, 0)[...].astype(F32) + self.end_l[dy].astype(F32) + self.end_r[dy].astype(F32)

        def send_y(self, dx):
            self.over_y[dx] = send(self.at(1, dx), self.box_y.at[dx], across)

        def add_y(self, dx):
            self.over_y[dx].wait_recv()
            mine = self.at(0, dx)
            mine[...] = (mine[...].astype(F32) + self.box_y[dx].astype(F32)).astype(BF16)

        def end_y(self):
            self.at(1, 0)[...] = self.x_sum(1).astype(BF16)
            self.over_y[0] = send(self.at(1, 0), self.box_y, across)

        def total(self):
            value = self.x_sum(0)
            if self.x_first:
                self.over_y[0].wait_recv()
                value = value + self.box_y[...].astype(F32)
            return value

    wx = Columns(part_w, 0, FIRST_X, True, boxes[0:5])
    wy = Columns(part_w, FIRST_X, units - FIRST_X, False, boxes[5:10])
    fx = Columns(part_f, 0, chunk, True, boxes[10:15])

    sets = {"w": wx, "v": wy, "f": fx}

    def multiply(slot):
        to_sibling[slot].wait_recv()
        left[slot, :, pl.ds(0, tokens)] = grad[:, share_of(slot, core)].T
        left[slot, :, pl.ds(tokens, tokens)] = grad_sib[slot].T

        @pl.loop(0, units // TILE)
        def _(n):
            tile = pl.ds(pl.multiple_of(n * TILE, TILE), TILE)
            part_w[slot, :, tile] = jnp.dot(left[slot], act[:, tile], preferred_element_type=F32).astype(BF16)

    def multiply_factor(slot):
        if slot == 0:
            cols["sibling"].wait_recv()
        value = jnp.dot(left[slot, :, pl.ds(0, tokens)], cols_own[...], preferred_element_type=F32)
        value = value + jnp.dot(left[slot, :, pl.ds(tokens, tokens)], cols_sib[...], preferred_element_type=F32)
        part_f[slot] = value.astype(BF16)

    def multiply_hidden(first, last):
        @pl.loop(first, last)
        def _(n):
            w_tile(n).wait()
            tile = pl.ds(pl.multiple_of(n * TILE, TILE), TILE)
            hidden[:, tile] = jnp.dot(grad[...], w[n % 2], preferred_element_type=F32).astype(BF16)

            @pl.when(n + 2 < units // TILE)
            def _():
                w_tile(n + 2).start()

    def send_x(name, slot):
        dy, dx = ORDER[slot]
        (None, sets[name].near_right, sets[name].far, sets[name].near_left)[dx](dy)

    def relay_x(name, slot):
        dy, dx = ORDER[slot]
        (None, sets[name].relay_right, None, sets[name].relay_left)[dx](dy)

    scale = 1.0 / math.sqrt(tokens * 16)

    def finish(name):
        if name == "f":
            factor[...] = fx.total() / (tokens * 16)
        else:
            wgrad[:, sets[name].cols] = (sets[name].total() * scale).astype(BF16)

    gather_y(0)
    gather_own(0)
    act_there = send(own_act, act.at[pl.ds(tokens, tokens)], sibling)
    for slot in range(1, CHIPS):
        gather_y(slot)
    own_here.wait()
    for n in range(2):
        w_tile(n).start()
    steps = {
        "own": gather_own, "z": gather_z, "sib": gather_sibling, "cols": cols_z, "colsib": cols_sibling,
        "mul": multiply, "fac": multiply_factor, "x": send_x, "relay": relay_x, "y": wy.send_y, "addy": wy.add_y,
        "endy": lambda name: sets[name].end_y(), "hid": multiply_hidden, "fin": finish,
    }
    first = True
    for name, *where in PLAN:
        if name == "mul" and first:
            act_here.wait()
            act_there.wait_recv()
            first = False
        steps[name](*where)
    hidden_done = move(hidden, hidden_out)
    wgrad_done = move(wgrad, wgrad_out)
    factor_done = move(factor, factor_out)
    for copy in remotes:
        copy.wait_send()
    for copy in (hidden_done, wgrad_done, factor_done):
        copy.wait()


def shards(out_grad, hidden_act, w_down):
    rows, width = out_grad.shape
    tokens, units = hidden_act.shape
    chunk = width // CHIPS
    share, half = chunk // 2, chunk // 4

    def boxes(count, x_first):
        ways = 2 if x_first else 1
        relay, end = pltpu.VMEM((ways, half, count), BF16), pltpu.VMEM((ways, share, count), BF16)
        over = pltpu.VMEM((share, count) if x_first else (4, share, count), BF16)
        return [relay, relay, end, end, over]

    def body(*refs):
        kernel(*refs[:18], refs[18:33], *refs[33:])

    return pl.pallas_call(
        body,
        out_shape=(
            jax.ShapeDtypeStruct((tokens, units), BF16),
            jax.ShapeDtypeStruct((share, units), BF16),
            jax.ShapeDtypeStruct((share, chunk), F32),
        ),
        in_specs=[pl.BlockSpec(memory_space=pl.ANY)] * 3,
        out_specs=(pl.BlockSpec(memory_space=pl.ANY),) * 3,
        scratch_shapes=[
            pltpu.VMEM((tokens, width), BF16),
            pltpu.VMEM((CHIPS, tokens, share), BF16),
            pltpu.VMEM((tokens, chunk), BF16),
            pltpu.VMEM((tokens, chunk), BF16),
            pltpu.VMEM((2 * tokens, units), BF16),
            pltpu.VMEM((2, width, TILE), BF16),
            pltpu.VMEM((CHIPS, share, 2 * tokens), BF16),
            pltpu.VMEM((CHIPS, share, units), BF16),
            pltpu.VMEM((CHIPS, share, chunk), BF16),
            pltpu.VMEM((tokens, units), BF16),
            pltpu.VMEM((share, units), BF16),
            pltpu.VMEM((share, chunk), F32),
            *boxes(FIRST_X, True),
            *boxes(units - FIRST_X, False),
            *boxes(chunk, True),
            pltpu.SemaphoreType.DMA((COPIES,)),
            pltpu.SemaphoreType.DMA((COPIES,)),
            pltpu.SemaphoreType.DMA((8,)),
            pltpu.SemaphoreType.DMA((2,)),
        ],
        compiler_params=pltpu.CompilerParams(
            collective_id=0, has_side_effects=True, vmem_limit_bytes=50 * 2**20),
    )(out_grad, hidden_act, w_down)


def solution(mesh):
    return jax.shard_map(
        shards,
        mesh=mesh,
        in_specs=(P(("dp", "tensor"), None), P("dp", "tensor"), P(None, "tensor")),
        out_specs=(P("dp", "tensor"), P("dp", "tensor"), P("dp", "tensor")),
        check_vma=False,
    )
```

```python
import math

import jax
import jax.numpy as jnp
from jax import lax
from jax.experimental import pallas as pl
from jax.experimental.pallas import tpu as pltpu
from jax.sharding import PartitionSpec as P

MESH = pl.DeviceIdType.MESH
BF16 = jnp.bfloat16
F32 = jnp.float32

ORDER = ((1, 2), (0, 2), (1, 1), (0, 3), (1, 3), (0, 1), (1, 0), (0, 0))
SLOT = {pair: slot for slot, pair in enumerate(ORDER)}
CHIPS = len(ORDER)
TILE = 256
SETS = {
    "wa": ("w", 0, 384, True),
    "wb": ("w", 384, 384, True),
    "va": ("w", 768, 512, False),
    "vb": ("w", 1280, 512, False),
    "f": ("f", 0, 512, True),
}
SPLIT = 768
COPIES = 160


EARLY = (0,)
RELAYED = (1, 2, 3, 4, 5, 6, 7)
PLAN = (
    ("z", 0), ("z", 1), ("z", 2), ("sib", 0), ("fwd", 1), ("z", 4), ("mul", 0), ("mulv", 0), ("y", "vb", 2),
    ("y", "va", 2), ("fwd", 2), ("z", 3), ("x", "wa", 0), ("sib", 1), ("x", "wb", 0), ("mul", 1), ("fwd", 4),
    ("z", 6), ("x", "wb", 1), ("sib", 2), ("z", 5), ("x", "wa", 1), ("mulv", 1), ("mul", 2), ("x", "wb", 2),
    ("x", "wa", 2), ("addy", "vb", 2), ("x", "vb", 1), ("sib", 4), ("fwd", 3), ("mulv", 2), ("y", "va", 1),
    ("mul", 4), ("x", "wa", 4), ("fwd", 6), ("relay", "wb", 4), ("mulv", 4), ("y", "vb", 3), ("x", "wb", 4),
    ("fwd", 5), ("addy", "va", 2), ("z", 7), ("cols",), ("relay", "wb", 2), ("relay", "wa", 2), ("sib", 3),
    ("relay", "wa", 4), ("sib", 6), ("y", "vb", 1), ("x", "va", 1), ("sib", 5), ("mul", 3), ("mulv", 3),
    ("x", "wa", 3), ("mul", 5), ("x", "wb", 5), ("relay", "wa", 3), ("relay", "wb", 3), ("relay", "wa", 5),
    ("fwd", 7), ("mul", 6), ("endy", "wb"), ("relay", "wb", 5), ("endy", "wa"), ("colsib",), ("addy", "vb", 3),
    ("x", "vb", 3), ("x", "wa", 5), ("mulv", 5), ("addy", "va", 1), ("fac", 0), ("x", "f", 0), ("fac", 2),
    ("x", "f", 2), ("sib", 7), ("fac", 3), ("addy", "vb", 1), ("fac", 4), ("x", "f", 3), ("fac", 6), ("y", "va", 3),
    ("x", "vb", 5), ("mulv", 6), ("fac", 1), ("x", "f", 1), ("y", "vb", 0), ("x", "f", 4), ("mul", 7),
    ("relay", "f", 2), ("y", "va", 0), ("x", "wb", 3), ("hid", 0, 1), ("relay", "f", 4), ("relay", "va", 5),
    ("fac", 5), ("x", "f", 5), ("relay", "vb", 5), ("relay", "vb", 3), ("hid", 1, 3), ("addy", "va", 3),
    ("x", "va", 3), ("relay", "va", 3), ("x", "va", 5), ("relay", "f", 3), ("hid", 3, 5), ("fin", "wb"),
    ("endy", "f"), ("hid", 5, 7), ("relay", "f", 5), ("mulv", 7), ("addy", "vb", 0), ("fin", "vb"), ("addy", "va", 0),
    ("fin", "va"), ("fin", "wa"), ("fac", 7), ("fin", "f"),
)


def kernel(own_grad, own_act, weight, hidden_out, wgrad_out, factor_out,
           grad, grad_sib, cols_own, cols_sib, act, w, left, part_w, part_f, hidden, wgrad, factor, boxes,
           send_sem, recv_sem, local_sem, w_sem):
    rows, width = own_grad.shape
    tokens, units = own_act.shape
    chunk = width // CHIPS
    share = chunk // 2
    half = share // 2
    dp, t = lax.axis_index("dp"), lax.axis_index("tensor")
    core, x, y = dp % 2, (dp // 2) % 4, dp // 8
    z, y_lo = t // 2, t % 2

    def on_x(step):
        return (y * 8 + ((x + step) % 4) * 2 + core, t)

    def on_z(step):
        return (dp, ((z + step) % 4) * 2 + y_lo)

    sibling = (dp + 1 - 2 * core, t)
    right, left_chip = on_x(1), on_x(3)
    across = ((1 - y) * 8 + x * 2 + core, t)
    partner = (dp, z * 2 + 1 - y_lo)
    along = (2, 1, 3)
    up, down = on_z(1), on_z(3)

    barrier = pltpu.get_barrier_semaphore()
    everyone = (sibling, right, left_chip, across, partner) + tuple(on_z(step) for step in along)
    for device in everyone:
        pl.semaphore_signal(barrier, inc=1, device_id=device, device_id_type=MESH)

    remotes, locals_, results = [], [], []

    def send(src, dst, device):
        number = len(remotes)
        copy = pltpu.make_async_remote_copy(
            src_ref=src, dst_ref=dst, send_sem=send_sem.at[number], recv_sem=recv_sem.at[number],
            device_id=device, device_id_type=MESH)
        copy.start()
        remotes.append(copy)
        return copy

    def move(src, dst):
        copy = pltpu.make_async_copy(src, dst, local_sem.at[len(locals_)])
        copy.start()
        locals_.append(copy)
        return copy

    def first_col(slot):
        dy, dx = ORDER[slot]
        return (((y + dy) % 2) * 4 + (x + dx) % 4) * chunk

    def columns(slot):
        return pl.ds(pl.multiple_of(first_col(slot), chunk), chunk)

    def share_of(slot, which):
        return pl.ds(pl.multiple_of(first_col(slot) + which * share, share), share)

    def columns_of(there):
        return pl.ds(pl.multiple_of(there * chunk, chunk), chunk)

    own_rows = pl.ds(pl.multiple_of(t * rows, rows), rows)
    partner_rows = pl.ds(pl.multiple_of((z * 2 + 1 - y_lo) * rows, rows), rows)
    pair_rows = pl.ds(pl.multiple_of(z * 2 * rows, 2 * rows), 2 * rows)

    def w_tile(n):
        cols = pl.ds(pl.multiple_of(n * TILE, TILE), TILE)
        return pltpu.make_async_copy(weight.at[:, cols], w.at[n % 2], w_sem.at[n % 2])

    own_here = move(own_grad, grad.at[own_rows, :])
    act_here = move(own_act, act.at[pl.ds(0, tokens)])
    pl.semaphore_wait(barrier, len(everyone))

    from_partner, along_z, to_sibling, cols = {}, {}, {}, {}

    def gather_y(slot):
        piece = columns(slot)
        from_partner[slot] = send(own_grad.at[:, piece], grad.at[own_rows, piece], partner)

    def gather_own(slot):
        piece = columns(slot)
        along_z[slot] = [send(own_grad.at[:, piece], grad.at[own_rows, piece], on_z(step)) for step in along]

    def gather_z(slot):
        from_partner[slot].wait_recv()
        piece = grad.at[partner_rows if slot in EARLY else pair_rows, columns(slot)]
        steps = (1, 3) if slot in RELAYED else along
        along_z.setdefault(slot, []).extend([send(piece, piece, on_z(step)) for step in steps])

    def forward_z(slot):
        copies = []
        for copy, step, low, device in zip(along_z[slot], (3, 1), (0, rows), (up, down)):
            copy.wait_recv()
            first = ((z + step) % 4) * 2 * rows + low
            piece = grad.at[pl.ds(pl.multiple_of(first, rows), rows), columns(slot)]
            copies.append(send(piece, piece, device))
        along_z[slot] = copies

    def gather_sibling(slot):
        for copy in along_z[slot]:
            copy.wait_recv()
        to_sibling[slot] = send(grad.at[:, share_of(slot, 1 - core)], grad_sib.at[slot], sibling)

    def cols_z():
        cols["here"] = move(grad.at[pair_rows, columns_of(t)], cols_own.at[pair_rows, :])
        cols["z"] = [
            send(grad.at[pair_rows, columns_of(((z + step) % 4) * 2 + y_lo)], cols_own.at[pair_rows, :], on_z(step))
            for step in along]

    def cols_sibling():
        cols["here"].wait()
        for copy in cols["z"]:
            copy.wait_recv()
        cols["sibling"] = send(cols_own, cols_sib, sibling)

    class Columns:
        def __init__(self, part, start, count, x_first, box):
            self.part, self.cols, self.x_first = part, pl.ds(start, count), x_first
            self.relay_l, self.relay_r, self.end_l, self.end_r, self.box_y = box
            self.relays, self.ends, self.over_y = {}, {}, {}

        def at(self, dy, dx, low=0, count=share):
            return self.part.at[SLOT[dy, dx], pl.ds(low, count), self.cols]

        def far(self, dy):
            self.relays[dy] = (
                send(self.at(dy, 2, 0, half), self.relay_l.at[dy], right),
                send(self.at(dy, 2, half, half), self.relay_r.at[dy], left_chip))

        def near_right(self, dy):
            self.ends[dy, 1, 1] = send(self.at(dy, 1, half, half), self.end_l.at[dy, pl.ds(half, half)], right)

        def near_left(self, dy):
            self.ends[dy, 3, 0] = send(self.at(dy, 3, 0, half), self.end_r.at[dy, pl.ds(0, half)], left_chip)

        def relay_right(self, dy):
            self.relays[dy][0].wait_recv()
            mine = self.at(dy, 1, 0, half)
            mine[...] = (mine[...].astype(F32) + self.relay_l[dy].astype(F32)).astype(BF16)
            self.ends[dy, 1, 0] = send(mine, self.end_l.at[dy, pl.ds(0, half)], right)

        def relay_left(self, dy):
            self.relays[dy][1].wait_recv()
            mine = self.at(dy, 3, half, half)
            mine[...] = (mine[...].astype(F32) + self.relay_r[dy].astype(F32)).astype(BF16)
            self.ends[dy, 3, 1] = send(mine, self.end_r.at[dy, pl.ds(half, half)], left_chip)

        def x_sum(self, dy):
            for place in ((1, 0), (1, 1), (3, 0), (3, 1)):
                self.ends[(dy,) + place].wait_recv()
            return self.at(dy, 0)[...].astype(F32) + self.end_l[dy].astype(F32) + self.end_r[dy].astype(F32)

        def send_y(self, dx):
            self.over_y[dx] = send(self.at(1, dx), self.box_y.at[dx], across)

        def add_y(self, dx):
            self.over_y[dx].wait_recv()
            mine = self.at(0, dx)
            mine[...] = (mine[...].astype(F32) + self.box_y[dx].astype(F32)).astype(BF16)

        def end_y(self):
            self.at(1, 0)[...] = self.x_sum(1).astype(BF16)
            self.over_y[0] = send(self.at(1, 0), self.box_y, across)

        def total(self):
            value = self.x_sum(0)
            if self.x_first:
                self.over_y[0].wait_recv()
                value = value + self.box_y[...].astype(F32)
            return value

    sets, parts = {}, {"w": part_w, "f": part_f}
    for number, (name, (part, start, count, x_first)) in enumerate(SETS.items()):
        sets[name] = Columns(parts[part], start, count, x_first, boxes[5 * number:5 * number + 5])

    def multiply(slot):
        to_sibling[slot].wait_recv()
        left[slot, :, pl.ds(0, tokens)] = grad[:, share_of(slot, core)].T
        left[slot, :, pl.ds(tokens, tokens)] = grad_sib[slot].T
        multiply_cols(slot, 0, SPLIT)

    def multiply_rest(slot):
        multiply_cols(slot, SPLIT, units)

    def multiply_cols(slot, start, end):
        def product(tile):
            part_w[slot, :, tile] = jnp.dot(left[slot], act[:, tile], preferred_element_type=F32).astype(BF16)

        full = (end - start) // TILE

        @pl.loop(0, full)
        def _(n):
            product(pl.ds(pl.multiple_of(start + n * TILE, TILE // 2), TILE))

        if start + full * TILE < end:
            product(pl.ds(start + full * TILE, end - start - full * TILE))

    def multiply_factor(slot):
        if slot == 0:
            cols["sibling"].wait_recv()
        value = jnp.dot(left[slot, :, pl.ds(0, tokens)], cols_own[...], preferred_element_type=F32)
        value = value + jnp.dot(left[slot, :, pl.ds(tokens, tokens)], cols_sib[...], preferred_element_type=F32)
        part_f[slot] = value.astype(BF16)

    def multiply_hidden(first, last):
        @pl.loop(first, last)
        def _(n):
            w_tile(n).wait()
            tile = pl.ds(pl.multiple_of(n * TILE, TILE), TILE)
            hidden[:, tile] = jnp.dot(grad[...], w[n % 2], preferred_element_type=F32).astype(BF16)

            @pl.when(n + 2 < units // TILE)
            def _():
                w_tile(n + 2).start()

        if last == units // TILE:
            results.append(move(hidden, hidden_out))

    def send_x(name, slot):
        dy, dx = ORDER[slot]
        (None, sets[name].near_right, sets[name].far, sets[name].near_left)[dx](dy)

    def relay_x(name, slot):
        dy, dx = ORDER[slot]
        (None, sets[name].relay_right, None, sets[name].relay_left)[dx](dy)

    scale = 1.0 / math.sqrt(tokens * 16)

    def finish(name):
        if SETS[name][0] == "f":
            factor[:, sets[name].cols] = sets[name].total() / (tokens * 16)
            results.append(move(factor.at[:, sets[name].cols], factor_out.at[:, sets[name].cols]))
        else:
            wgrad[:, sets[name].cols] = (sets[name].total() * scale).astype(BF16)
            results.append(move(wgrad.at[:, sets[name].cols], wgrad_out.at[:, sets[name].cols]))

    gather_y(0)
    gather_own(0)
    act_there = send(own_act, act.at[pl.ds(tokens, tokens)], sibling)
    for slot in range(1, CHIPS):
        gather_y(slot)
    own_here.wait()
    for n in range(2):
        w_tile(n).start()
    steps = {
        "own": gather_own, "z": gather_z, "sib": gather_sibling, "cols": cols_z, "colsib": cols_sibling,
        "fwd": forward_z, "mul": multiply, "mulv": multiply_rest, "fac": multiply_factor, "x": send_x, "relay": relay_x,
        "y": lambda name, dx: sets[name].send_y(dx), "addy": lambda name, dx: sets[name].add_y(dx),
        "endy": lambda name: sets[name].end_y(), "hid": multiply_hidden, "fin": finish,
    }
    first = True
    for name, *where in PLAN:
        if name == "mul" and first:
            act_here.wait()
            act_there.wait_recv()
            first = False
        steps[name](*where)
    for copy in remotes:
        copy.wait_send()
    for copy in results:
        copy.wait()


def shards(out_grad, hidden_act, w_down):
    rows, width = out_grad.shape
    tokens, units = hidden_act.shape
    chunk = width // CHIPS
    share, half = chunk // 2, chunk // 4

    def boxes(count, x_first):
        ways = 2 if x_first else 1
        relay, end = pltpu.VMEM((ways, half, count), BF16), pltpu.VMEM((ways, share, count), BF16)
        over = pltpu.VMEM((share, count) if x_first else (4, share, count), BF16)
        return [relay, relay, end, end, over]

    def body(*refs):
        kernel(*refs[:18], refs[18:-4], *refs[-4:])

    return publish(*pl.pallas_call(
        body,
        out_shape=(
            jax.ShapeDtypeStruct((tokens, units), BF16),
            jax.ShapeDtypeStruct((share, units), BF16),
            jax.ShapeDtypeStruct((share, chunk), F32),
        ),
        in_specs=[pl.BlockSpec(memory_space=pl.ANY)] * 3,
        out_specs=(pl.BlockSpec(memory_space=pl.ANY),) * 3,
        scratch_shapes=[
            pltpu.VMEM((tokens, width), BF16),
            pltpu.VMEM((CHIPS, tokens, share), BF16),
            pltpu.VMEM((tokens, chunk), BF16),
            pltpu.VMEM((tokens, chunk), BF16),
            pltpu.VMEM((2 * tokens, units), BF16),
            pltpu.VMEM((2, width, TILE), BF16),
            pltpu.VMEM((CHIPS, share, 2 * tokens), BF16),
            pltpu.VMEM((CHIPS, share, units), BF16),
            pltpu.VMEM((CHIPS, share, chunk), BF16),
            pltpu.VMEM((tokens, units), BF16),
            pltpu.VMEM((share, units), BF16),
            pltpu.VMEM((share, chunk), F32),
            *[box for _, _, count, x_first in SETS.values() for box in boxes(count, x_first)],
            pltpu.SemaphoreType.DMA((COPIES,)),
            pltpu.SemaphoreType.DMA((COPIES,)),
            pltpu.SemaphoreType.DMA((16,)),
            pltpu.SemaphoreType.DMA((2,)),
        ],
        compiler_params=pltpu.CompilerParams(
            collective_id=0, has_side_effects=True, vmem_limit_bytes=50 * 2**20),
    )(out_grad, hidden_act, w_down))


def publish(hidden, wgrad, factor):
    def body(*refs):
        sems = refs[6]
        copies = [pltpu.make_async_copy(refs[i], refs[3 + i], sems.at[i]) for i in range(3)]
        for copy in copies:
            copy.start()
        for copy in copies:
            copy.wait()

    return pl.pallas_call(
        body,
        out_shape=tuple(jax.ShapeDtypeStruct(a.shape, a.dtype) for a in (hidden, wgrad, factor)),
        in_specs=[pl.BlockSpec(memory_space=pl.ANY)] * 3,
        out_specs=(pl.BlockSpec(memory_space=pl.ANY),) * 3,
        scratch_shapes=[pltpu.SemaphoreType.DMA((3,))],
        compiler_params=pltpu.CompilerParams(vmem_limit_bytes=2**20),
    )(hidden, wgrad, factor)


def solution(mesh):
    return jax.shard_map(
        shards,
        mesh=mesh,
        in_specs=(P(("dp", "tensor"), None), P("dp", "tensor"), P(None, "tensor")),
        out_specs=(P("dp", "tensor"), P("dp", "tensor"), P("dp", "tensor")),
        check_vma=False,
    )
```

```python
import math

import jax
import jax.numpy as jnp
from jax import lax
from jax.experimental import pallas as pl
from jax.experimental.pallas import tpu as pltpu
from jax.sharding import PartitionSpec as P

MESH = pl.DeviceIdType.MESH
BF16 = jnp.bfloat16
F32 = jnp.float32

ORDER = ((1, 2), (0, 2), (1, 1), (1, 3), (1, 0), (0, 3), (0, 1), (0, 0))
SLOT = {pair: slot for slot, pair in enumerate(ORDER)}
CHIPS = len(ORDER)
TILE = 256
SETS = {
    "wa": ("w", 0, 256, True),
    "wb": ("w", 256, 512, True),
    "va": ("w", 768, 512, False),
    "vb": ("w", 1280, 256, False),
    "vc": ("w", 1536, 256, False),
    "fa": ("f", 0, 512, True),
}
SPLIT = 768
COPIES = 160


EARLY = (0,)
RELAYED = (1, 2, 3, 4, 5, 6, 7)
PLAN = (
    ("yw", 0), ("z", 0), ("yw", 1), ("z", 1), ("yw", 3), ("yw", 2), ("z", 2), ("sib", 0), ("fwd", 1), ("z", 3),
    ("mul", 0), ("mulv", 0), ("y", "va", 2), ("x", "wa", 0), ("fwd", 2), ("sib", 1), ("yw", 6), ("z", 6),
    ("x", "wb", 0), ("y", "vc", 2), ("yw", 5), ("mul", 1), ("x", "wb", 1), ("y", "vb", 2), ("fwd", 3), ("sib", 2),
    ("z", 5), ("mulv", 1), ("x", "wa", 1), ("mul", 2), ("addy", "va", 2), ("x", "va", 1), ("yw", 4), ("z", 4),
    ("sib", 3), ("mulv", 2), ("y", "vb", 1), ("y", "vc", 1), ("relay", "wb", 2), ("fwd", 6), ("addy", "vc", 2),
    ("x", "vc", 1), ("mul", 3), ("x", "wb", 3), ("x", "wa", 2), ("relay", "wa", 2), ("relay", "wb", 3), ("fwd", 5),
    ("mulv", 3), ("y", "vc", 3), ("relay", "wa", 3), ("addy", "vb", 2), ("fwd", 4), ("x", "wb", 2), ("yw", 7),
    ("cols",), ("x", "vb", 1), ("sib", 6), ("y", "vb", 3), ("sib", 5), ("mul", 6), ("x", "wb", 6), ("x", "wa", 6),
    ("sib", 4), ("y", "va", 3), ("x", "wa", 3), ("z", 7), ("mul", 5), ("relay", "wa", 5), ("mulv", 5), ("mul", 4),
    ("x", "wb", 5), ("relay", "wb", 6), ("mulv", 6), ("x", "wa", 5), ("addy", "vc", 1), ("colsib",), ("endy", "wb"),
    ("addy", "vb", 3), ("relay", "vc", 6), ("x", "vb", 5), ("addy", "vc", 3), ("y", "va", 1), ("mulv", 4),
    ("relay", "wb", 5), ("y", "vb", 0), ("fwd", 7), ("fac", 0), ("x", "fa", 0), ("fac", 1), ("x", "fa", 1),
    ("relay", "vc", 5), ("addy", "vb", 1), ("x", "vb", 6), ("relay", "vb", 6), ("x", "vc", 5), ("fac", 2),
    ("x", "fa", 2), ("x", "vc", 6), ("y", "vc", 0), ("fac", 3), ("x", "fa", 3), ("relay", "wa", 6), ("endy", "wa"),
    ("relay", "vb", 5), ("sib", 7), ("hid", 0, 3), ("y", "va", 0), ("relay", "fa", 3), ("addy", "va", 3),
    ("hid", 3, 4), ("relay", "fa", 2), ("hid", 4, 5), ("addy", "va", 1), ("x", "va", 6), ("x", "va", 5),
    ("relay", "va", 6), ("mul", 7), ("fac", 7), ("mulv", 7), ("addy", "vb", 0), ("fin", "vb"), ("fac", 5),
    ("relay", "va", 5), ("relay", "fa", 5), ("fac", 4), ("endy", "fa"), ("addy", "vc", 0), ("fac", 6), ("x", "fa", 6),
    ("relay", "fa", 6), ("fin", "vc"), ("fin", "wa"), ("x", "fa", 5), ("fin", "wb"), ("hid", 5, 7), ("addy", "va", 0),
    ("fin", "va"), ("fin", "fa"),
)


def kernel(own_grad, own_act, weight, hidden_out, wgrad_out, factor_out,
           grad, grad_sib, cols_own, cols_sib, act, w, left, part_w, part_f, hidden, wgrad, factor, boxes,
           send_sem, recv_sem, local_sem, w_sem):
    rows, width = own_grad.shape
    tokens, units = own_act.shape
    chunk = width // CHIPS
    share = chunk // 2
    half = share // 2
    dp, t = lax.axis_index("dp"), lax.axis_index("tensor")
    core, x, y = dp % 2, (dp // 2) % 4, dp // 8
    z, y_lo = t // 2, t % 2

    def on_x(step):
        return (y * 8 + ((x + step) % 4) * 2 + core, t)

    def on_z(step):
        return (dp, ((z + step) % 4) * 2 + y_lo)

    sibling = (dp + 1 - 2 * core, t)
    right, left_chip = on_x(1), on_x(3)
    across = ((1 - y) * 8 + x * 2 + core, t)
    partner = (dp, z * 2 + 1 - y_lo)
    along = (2, 1, 3)
    up, down = on_z(1), on_z(3)

    barrier = pltpu.get_barrier_semaphore()
    everyone = (sibling, right, left_chip, across, partner) + tuple(on_z(step) for step in along)
    for device in everyone:
        pl.semaphore_signal(barrier, inc=1, device_id=device, device_id_type=MESH)

    remotes, locals_, results = [], [], []

    def send(src, dst, device):
        number = len(remotes)
        copy = pltpu.make_async_remote_copy(
            src_ref=src, dst_ref=dst, send_sem=send_sem.at[number], recv_sem=recv_sem.at[number],
            device_id=device, device_id_type=MESH)
        copy.start()
        remotes.append(copy)
        return copy

    def move(src, dst):
        copy = pltpu.make_async_copy(src, dst, local_sem.at[len(locals_)])
        copy.start()
        locals_.append(copy)
        return copy

    def first_col(slot):
        dy, dx = ORDER[slot]
        return (((y + dy) % 2) * 4 + (x + dx) % 4) * chunk

    def columns(slot):
        return pl.ds(pl.multiple_of(first_col(slot), chunk), chunk)

    def share_of(slot, which):
        return pl.ds(pl.multiple_of(first_col(slot) + which * share, share), share)

    def columns_of(there):
        return pl.ds(pl.multiple_of(there * chunk, chunk), chunk)

    own_rows = pl.ds(pl.multiple_of(t * rows, rows), rows)
    partner_rows = pl.ds(pl.multiple_of((z * 2 + 1 - y_lo) * rows, rows), rows)
    pair_rows = pl.ds(pl.multiple_of(z * 2 * rows, 2 * rows), 2 * rows)

    def w_tile(n):
        cols = pl.ds(pl.multiple_of(n * TILE, TILE), TILE)
        return pltpu.make_async_copy(weight.at[:, cols], w.at[n % 2], w_sem.at[n % 2])

    own_here = move(own_grad, grad.at[own_rows, :])
    act_here = move(own_act, act.at[pl.ds(0, tokens)])
    pl.semaphore_wait(barrier, len(everyone))

    from_partner, along_z, to_sibling, cols = {}, {}, {}, {}

    def gather_y(slot):
        piece = columns(slot)
        from_partner[slot] = send(own_grad.at[:, piece], grad.at[own_rows, piece], partner)

    def gather_own(slot):
        piece = columns(slot)
        along_z[slot] = [send(own_grad.at[:, piece], grad.at[own_rows, piece], on_z(step)) for step in along]

    def wait_y(slot):
        from_partner[slot].wait_recv()

    def gather_z(slot):
        piece = grad.at[partner_rows if slot in EARLY else pair_rows, columns(slot)]
        steps = (1, 3) if slot in RELAYED else along
        along_z.setdefault(slot, []).extend([send(piece, piece, on_z(step)) for step in steps])

    def forward_z(slot):
        copies = []
        for copy, step, low, device in zip(along_z[slot], (3, 1), (0, rows), (up, down)):
            copy.wait_recv()
            first = ((z + step) % 4) * 2 * rows + low
            piece = grad.at[pl.ds(pl.multiple_of(first, rows), rows), columns(slot)]
            copies.append(send(piece, piece, device))
        along_z[slot] = copies

    def gather_sibling(slot):
        for copy in along_z[slot]:
            copy.wait_recv()
        to_sibling[slot] = send(grad.at[:, share_of(slot, 1 - core)], grad_sib.at[slot], sibling)

    def cols_z():
        cols["here"] = move(grad.at[pair_rows, columns_of(t)], cols_own.at[pair_rows, :])
        cols["z"] = [
            send(grad.at[pair_rows, columns_of(((z + step) % 4) * 2 + y_lo)], cols_own.at[pair_rows, :], on_z(step))
            for step in along]

    def cols_sibling():
        cols["here"].wait()
        for copy in cols["z"]:
            copy.wait_recv()
        cols["sibling"] = send(cols_own, cols_sib, sibling)

    class Columns:
        def __init__(self, part, start, count, x_first, box):
            self.part, self.cols, self.x_first = part, pl.ds(start, count), x_first
            self.relay_l, self.relay_r, self.end_l, self.end_r, self.box_y = box
            self.relays, self.ends, self.over_y = {}, {}, {}

        def at(self, dy, dx, low=0, count=share):
            return self.part.at[SLOT[dy, dx], pl.ds(low, count), self.cols]

        def far(self, dy):
            self.relays[dy] = (
                send(self.at(dy, 2, 0, half), self.relay_l.at[dy], right),
                send(self.at(dy, 2, half, half), self.relay_r.at[dy], left_chip))

        def near_right(self, dy):
            self.ends[dy, 1, 1] = send(self.at(dy, 1, half, half), self.end_l.at[dy, pl.ds(half, half)], right)

        def near_left(self, dy):
            self.ends[dy, 3, 0] = send(self.at(dy, 3, 0, half), self.end_r.at[dy, pl.ds(0, half)], left_chip)

        def relay_right(self, dy):
            self.relays[dy][0].wait_recv()
            mine = self.at(dy, 1, 0, half)
            mine[...] = (mine[...].astype(F32) + self.relay_l[dy].astype(F32)).astype(BF16)
            self.ends[dy, 1, 0] = send(mine, self.end_l.at[dy, pl.ds(0, half)], right)

        def relay_left(self, dy):
            self.relays[dy][1].wait_recv()
            mine = self.at(dy, 3, half, half)
            mine[...] = (mine[...].astype(F32) + self.relay_r[dy].astype(F32)).astype(BF16)
            self.ends[dy, 3, 1] = send(mine, self.end_r.at[dy, pl.ds(half, half)], left_chip)

        def x_sum(self, dy):
            for place in ((1, 0), (1, 1), (3, 0), (3, 1)):
                self.ends[(dy,) + place].wait_recv()
            return self.at(dy, 0)[...].astype(F32) + self.end_l[dy].astype(F32) + self.end_r[dy].astype(F32)

        def send_y(self, dx):
            self.over_y[dx] = send(self.at(1, dx), self.box_y.at[dx], across)

        def add_y(self, dx):
            self.over_y[dx].wait_recv()
            mine = self.at(0, dx)
            mine[...] = (mine[...].astype(F32) + self.box_y[dx].astype(F32)).astype(BF16)

        def end_y(self):
            self.at(1, 0)[...] = self.x_sum(1).astype(BF16)
            self.over_y[0] = send(self.at(1, 0), self.box_y, across)

        def total(self):
            value = self.x_sum(0)
            if self.x_first:
                self.over_y[0].wait_recv()
                value = value + self.box_y[...].astype(F32)
            return value

    sets, parts = {}, {"w": part_w, "f": part_f}
    for number, (name, (part, start, count, x_first)) in enumerate(SETS.items()):
        sets[name] = Columns(parts[part], start, count, x_first, boxes[5 * number:5 * number + 5])

    def multiply(slot):
        to_sibling[slot].wait_recv()
        left[slot, :, pl.ds(0, tokens)] = grad[:, share_of(slot, core)].T
        left[slot, :, pl.ds(tokens, tokens)] = grad_sib[slot].T
        multiply_cols(slot, 0, SPLIT)

    def multiply_rest(slot):
        multiply_cols(slot, SPLIT, units)

    def multiply_cols(slot, start, end):
        def product(tile):
            part_w[slot, :, tile] = jnp.dot(left[slot], act[:, tile], preferred_element_type=F32).astype(BF16)

        full = (end - start) // TILE

        @pl.loop(0, full)
        def _(n):
            product(pl.ds(pl.multiple_of(start + n * TILE, TILE // 2), TILE))

        if start + full * TILE < end:
            product(pl.ds(start + full * TILE, end - start - full * TILE))

    def multiply_factor(slot):
        if slot == 0:
            cols["sibling"].wait_recv()
        value = jnp.dot(left[slot, :, pl.ds(0, tokens)], cols_own[...], preferred_element_type=F32)
        value = value + jnp.dot(left[slot, :, pl.ds(tokens, tokens)], cols_sib[...], preferred_element_type=F32)
        part_f[slot] = value.astype(BF16)

    def multiply_hidden(first, last):
        @pl.loop(first, last)
        def _(n):
            w_tile(n).wait()
            tile = pl.ds(pl.multiple_of(n * TILE, TILE), TILE)
            hidden[:, tile] = jnp.dot(grad[...], w[n % 2], preferred_element_type=F32).astype(BF16)

            @pl.when(n + 2 < units // TILE)
            def _():
                w_tile(n + 2).start()

        if last == units // TILE:
            results.append(move(hidden, hidden_out))

    def send_x(name, slot):
        dy, dx = ORDER[slot]
        (None, sets[name].near_right, sets[name].far, sets[name].near_left)[dx](dy)

    def relay_x(name, slot):
        dy, dx = ORDER[slot]
        (None, sets[name].relay_right, None, sets[name].relay_left)[dx](dy)

    scale = 1.0 / math.sqrt(tokens * 16)

    def finish(name):
        if SETS[name][0] == "f":
            factor[:, sets[name].cols] = sets[name].total() / (tokens * 16)
            results.append(move(factor.at[:, sets[name].cols], factor_out.at[:, sets[name].cols]))
        else:
            wgrad[:, sets[name].cols] = (sets[name].total() * scale).astype(BF16)
            results.append(move(wgrad.at[:, sets[name].cols], wgrad_out.at[:, sets[name].cols]))

    gather_y(0)
    gather_own(0)
    act_there = send(own_act, act.at[pl.ds(tokens, tokens)], sibling)
    for slot in range(1, CHIPS):
        gather_y(slot)
    own_here.wait()
    for n in range(2):
        w_tile(n).start()
    steps = {
        "yw": wait_y, "own": gather_own, "z": gather_z, "sib": gather_sibling, "cols": cols_z, "colsib": cols_sibling,
        "fwd": forward_z, "mul": multiply, "mulv": multiply_rest, "fac": multiply_factor, "x": send_x, "relay": relay_x,
        "y": lambda name, dx: sets[name].send_y(dx), "addy": lambda name, dx: sets[name].add_y(dx),
        "endy": lambda name: sets[name].end_y(), "hid": multiply_hidden, "fin": finish,
    }
    first = True
    drained = 0
    for step, (name, *where) in enumerate(PLAN):
        if name == "mul" and first:
            act_here.wait()
            act_there.wait_recv()
            first = False
        steps[name](*where)
        if name in ("hid", "endy", "fin") and step > len(PLAN) // 2:
            upto = max(drained, len(remotes) - 20)
            for copy in remotes[drained:upto]:
                copy.wait_send()
            drained = upto
    for copy in remotes[drained:]:
        copy.wait_send()
    for copy in results:
        copy.wait()


def shards(out_grad, hidden_act, w_down):
    rows, width = out_grad.shape
    tokens, units = hidden_act.shape
    chunk = width // CHIPS
    share, half = chunk // 2, chunk // 4

    def boxes(count, x_first):
        ways = 2 if x_first else 1
        relay, end = pltpu.VMEM((ways, half, count), BF16), pltpu.VMEM((ways, share, count), BF16)
        over = pltpu.VMEM((share, count) if x_first else (4, share, count), BF16)
        return [relay, relay, end, end, over]

    def body(*refs):
        kernel(*refs[:18], refs[18:-4], *refs[-4:])

    return publish(*pl.pallas_call(
        body,
        out_shape=(
            jax.ShapeDtypeStruct((tokens, units), BF16),
            jax.ShapeDtypeStruct((share, units), BF16),
            jax.ShapeDtypeStruct((share, chunk), F32),
        ),
        in_specs=[pl.BlockSpec(memory_space=pl.ANY)] * 3,
        out_specs=(pl.BlockSpec(memory_space=pl.ANY),) * 3,
        scratch_shapes=[
            pltpu.VMEM((tokens, width), BF16),
            pltpu.VMEM((CHIPS, tokens, share), BF16),
            pltpu.VMEM((tokens, chunk), BF16),
            pltpu.VMEM((tokens, chunk), BF16),
            pltpu.VMEM((2 * tokens, units), BF16),
            pltpu.VMEM((2, width, TILE), BF16),
            pltpu.VMEM((CHIPS, share, 2 * tokens), BF16),
            pltpu.VMEM((CHIPS, share, units), BF16),
            pltpu.VMEM((CHIPS, share, chunk), BF16),
            pltpu.VMEM((tokens, units), BF16),
            pltpu.VMEM((share, units), BF16),
            pltpu.VMEM((share, chunk), F32),
            *[box for _, _, count, x_first in SETS.values() for box in boxes(count, x_first)],
            pltpu.SemaphoreType.DMA((COPIES,)),
            pltpu.SemaphoreType.DMA((COPIES,)),
            pltpu.SemaphoreType.DMA((16,)),
            pltpu.SemaphoreType.DMA((2,)),
        ],
        compiler_params=pltpu.CompilerParams(
            collective_id=0, has_side_effects=True, vmem_limit_bytes=50 * 2**20),
    )(out_grad, hidden_act, w_down))


def publish(hidden, wgrad, factor):
    def body(*refs):
        sems = refs[6]
        copies = [pltpu.make_async_copy(refs[i], refs[3 + i], sems.at[i]) for i in range(3)]
        for copy in copies:
            copy.start()
        for copy in copies:
            copy.wait()

    return pl.pallas_call(
        body,
        out_shape=tuple(jax.ShapeDtypeStruct(a.shape, a.dtype) for a in (hidden, wgrad, factor)),
        in_specs=[pl.BlockSpec(memory_space=pl.ANY)] * 3,
        out_specs=(pl.BlockSpec(memory_space=pl.ANY),) * 3,
        scratch_shapes=[pltpu.SemaphoreType.DMA((3,))],
        compiler_params=pltpu.CompilerParams(vmem_limit_bytes=2**20),
    )(hidden, wgrad, factor)


def solution(mesh):
    return jax.shard_map(
        shards,
        mesh=mesh,
        in_specs=(P(("dp", "tensor"), None), P("dp", "tensor"), P(None, "tensor")),
        out_specs=(P("dp", "tensor"), P("dp", "tensor"), P("dp", "tensor")),
        check_vma=False,
    )
```

```python
import math

import jax
import jax.numpy as jnp
from jax import lax
from jax.experimental import pallas as pl
from jax.experimental.pallas import tpu as pltpu
from jax.sharding import PartitionSpec as P

MESH = pl.DeviceIdType.MESH
BF16 = jnp.bfloat16
F32 = jnp.float32

ORDER = ((1, 2), (0, 2), (1, 1), (1, 3), (1, 0), (0, 3), (0, 1), (0, 0))
SLOT = {pair: slot for slot, pair in enumerate(ORDER)}
CHIPS = len(ORDER)
TILE = 256
SETS = {
    "wa": ("w", 0, 256, True),
    "wb": ("w", 256, 512, True),
    "va": ("w", 768, 512, False),
    "vb": ("w", 1280, 256, False),
    "vc": ("w", 1536, 256, False),
    "fa": ("f", 0, 512, True),
}
SPLIT = 768
FIRST_SENT = 256
COPIES = 160


EARLY = (0,)
RELAYED = (1, 2, 3, 4, 5, 6, 7)
PLAN = (
    ("yw", 0), ("z", 0), ("yw", 1), ("z", 1), ("yw", 3), ("yw", 2), ("z", 2), ("sib", 0), ("fwd", 1), ("z", 3),
    ("mul", 0), ("x", "wa", 0), ("mulb", 0),
    ("x", "wb", 0), ("mulv", 0), ("y", "va", 2), ("fwd", 2), ("sib", 1), ("yw", 6), ("z", 6),
    ("y", "vc", 2), ("yw", 5), ("mul", 1), ("x", "wb", 1), ("y", "vb", 2), ("fwd", 3), ("sib", 2),
    ("z", 5), ("mulv", 1), ("x", "wa", 1), ("mul", 2), ("addy", "va", 2), ("x", "va", 1), ("yw", 4), ("z", 4),
    ("sib", 3), ("mulv", 2), ("y", "vb", 1), ("y", "vc", 1), ("relay", "wb", 2), ("fwd", 6), ("addy", "vc", 2),
    ("x", "vc", 1), ("mul", 3), ("x", "wb", 3), ("x", "wa", 2), ("relay", "wa", 2), ("relay", "wb", 3), ("fwd", 5),
    ("mulv", 3), ("y", "vc", 3), ("relay", "wa", 3), ("addy", "vb", 2), ("fwd", 4), ("x", "wb", 2), ("yw", 7),
    ("cols",), ("x", "vb", 1), ("sib", 6), ("y", "vb", 3), ("sib", 5), ("mul", 6), ("x", "wb", 6), ("x", "wa", 6),
    ("sib", 4), ("y", "va", 3), ("x", "wa", 3), ("z", 7), ("mul", 5), ("relay", "wa", 5), ("mulv", 5), ("mul", 4),
    ("x", "wb", 5), ("relay", "wb", 6), ("mulv", 6), ("x", "wa", 5), ("addy", "vc", 1), ("colsib",), ("endy", "wb"),
    ("addy", "vb", 3), ("relay", "vc", 6), ("x", "vb", 5), ("addy", "vc", 3), ("y", "va", 1), ("mulv", 4),
    ("relay", "wb", 5), ("y", "vb", 0), ("fwd", 7), ("fac", 0), ("x", "fa", 0), ("fac", 1), ("x", "fa", 1),
    ("relay", "vc", 5), ("addy", "vb", 1), ("x", "vb", 6), ("relay", "vb", 6), ("x", "vc", 5), ("fac", 2),
    ("x", "fa", 2), ("x", "vc", 6), ("y", "vc", 0), ("fac", 3), ("x", "fa", 3), ("relay", "wa", 6), ("endy", "wa"),
    ("relay", "vb", 5), ("sib", 7), ("hid", 0, 3), ("y", "va", 0), ("relay", "fa", 3), ("addy", "va", 3),
    ("hid", 3, 4), ("relay", "fa", 2), ("hid", 4, 5), ("addy", "va", 1), ("x", "va", 6), ("x", "va", 5),
    ("relay", "va", 6), ("mul", 7), ("fac", 7), ("mulv", 7), ("addy", "vb", 0), ("fin", "vb"), ("fac", 5),
    ("relay", "va", 5), ("relay", "fa", 5), ("fac", 4), ("endy", "fa"), ("addy", "vc", 0), ("fac", 6), ("x", "fa", 6),
    ("relay", "fa", 6), ("fin", "vc"), ("fin", "wa"), ("x", "fa", 5), ("fin", "wb"), ("hid", 5, 7), ("addy", "va", 0),
    ("fin", "va"), ("fin", "fa"),
)


def kernel(own_grad, own_act, weight, hidden_out, wgrad_out, factor_out,
           grad, grad_sib, cols_own, cols_sib, act, w, left, part_w, part_f, hidden, wgrad, factor, boxes,
           send_sem, recv_sem, local_sem, w_sem):
    rows, width = own_grad.shape
    tokens, units = own_act.shape
    chunk = width // CHIPS
    share = chunk // 2
    half = share // 2
    dp, t = lax.axis_index("dp"), lax.axis_index("tensor")
    core, x, y = dp % 2, (dp // 2) % 4, dp // 8
    z, y_lo = t // 2, t % 2

    def on_x(step):
        return (y * 8 + ((x + step) % 4) * 2 + core, t)

    def on_z(step):
        return (dp, ((z + step) % 4) * 2 + y_lo)

    sibling = (dp + 1 - 2 * core, t)
    right, left_chip = on_x(1), on_x(3)
    across = ((1 - y) * 8 + x * 2 + core, t)
    partner = (dp, z * 2 + 1 - y_lo)
    along = (2, 1, 3)
    up, down = on_z(1), on_z(3)

    barrier = pltpu.get_barrier_semaphore()
    everyone = (sibling, right, left_chip, across, partner) + tuple(on_z(step) for step in along)
    for device in everyone:
        pl.semaphore_signal(barrier, inc=1, device_id=device, device_id_type=MESH)

    remotes, locals_, results = [], [], []

    def send(src, dst, device):
        number = len(remotes)
        copy = pltpu.make_async_remote_copy(
            src_ref=src, dst_ref=dst, send_sem=send_sem.at[number], recv_sem=recv_sem.at[number],
            device_id=device, device_id_type=MESH)
        copy.start()
        remotes.append(copy)
        return copy

    def move(src, dst):
        copy = pltpu.make_async_copy(src, dst, local_sem.at[len(locals_)])
        copy.start()
        locals_.append(copy)
        return copy

    def first_col(slot):
        dy, dx = ORDER[slot]
        return (((y + dy) % 2) * 4 + (x + dx) % 4) * chunk

    def columns(slot):
        return pl.ds(pl.multiple_of(first_col(slot), chunk), chunk)

    def share_of(slot, which):
        return pl.ds(pl.multiple_of(first_col(slot) + which * share, share), share)

    def columns_of(there):
        return pl.ds(pl.multiple_of(there * chunk, chunk), chunk)

    own_rows = pl.ds(pl.multiple_of(t * rows, rows), rows)
    partner_rows = pl.ds(pl.multiple_of((z * 2 + 1 - y_lo) * rows, rows), rows)
    pair_rows = pl.ds(pl.multiple_of(z * 2 * rows, 2 * rows), 2 * rows)

    def w_tile(n):
        cols = pl.ds(pl.multiple_of(n * TILE, TILE), TILE)
        return pltpu.make_async_copy(weight.at[:, cols], w.at[n % 2], w_sem.at[n % 2])

    own_here = move(own_grad, grad.at[own_rows, :])
    act_here = move(own_act, act.at[pl.ds(0, tokens)])
    pl.semaphore_wait(barrier, len(everyone))

    from_partner, along_z, to_sibling, cols = {}, {}, {}, {}

    def gather_y(slot):
        piece = columns(slot)
        from_partner[slot] = send(own_grad.at[:, piece], grad.at[own_rows, piece], partner)

    def gather_own(slot):
        piece = columns(slot)
        along_z[slot] = [send(own_grad.at[:, piece], grad.at[own_rows, piece], on_z(step)) for step in along]

    def wait_y(slot):
        from_partner[slot].wait_recv()

    def gather_z(slot):
        piece = grad.at[partner_rows if slot in EARLY else pair_rows, columns(slot)]
        steps = (1, 3) if slot in RELAYED else along
        along_z.setdefault(slot, []).extend([send(piece, piece, on_z(step)) for step in steps])

    def forward_z(slot):
        copies = []
        for copy, step, low, device in zip(along_z[slot], (3, 1), (0, rows), (up, down)):
            copy.wait_recv()
            first = ((z + step) % 4) * 2 * rows + low
            piece = grad.at[pl.ds(pl.multiple_of(first, rows), rows), columns(slot)]
            copies.append(send(piece, piece, device))
        along_z[slot] = copies

    def gather_sibling(slot):
        for copy in along_z[slot]:
            copy.wait_recv()
        to_sibling[slot] = send(grad.at[:, share_of(slot, 1 - core)], grad_sib.at[slot], sibling)

    def cols_z():
        cols["here"] = move(grad.at[pair_rows, columns_of(t)], cols_own.at[pair_rows, :])
        cols["z"] = [
            send(grad.at[pair_rows, columns_of(((z + step) % 4) * 2 + y_lo)], cols_own.at[pair_rows, :], on_z(step))
            for step in along]

    def cols_sibling():
        cols["here"].wait()
        for copy in cols["z"]:
            copy.wait_recv()
        cols["sibling"] = send(cols_own, cols_sib, sibling)

    class Columns:
        def __init__(self, part, start, count, x_first, box):
            self.part, self.cols, self.x_first = part, pl.ds(start, count), x_first
            self.relay_l, self.relay_r, self.end_l, self.end_r, self.box_y = box
            self.relays, self.ends, self.over_y = {}, {}, {}

        def at(self, dy, dx, low=0, count=share):
            return self.part.at[SLOT[dy, dx], pl.ds(low, count), self.cols]

        def far(self, dy):
            self.relays[dy] = (
                send(self.at(dy, 2, 0, half), self.relay_l.at[dy], right),
                send(self.at(dy, 2, half, half), self.relay_r.at[dy], left_chip))

        def near_right(self, dy):
            self.ends[dy, 1, 1] = send(self.at(dy, 1, half, half), self.end_l.at[dy, pl.ds(half, half)], right)

        def near_left(self, dy):
            self.ends[dy, 3, 0] = send(self.at(dy, 3, 0, half), self.end_r.at[dy, pl.ds(0, half)], left_chip)

        def relay_right(self, dy):
            self.relays[dy][0].wait_recv()
            mine = self.at(dy, 1, 0, half)
            mine[...] = (mine[...].astype(F32) + self.relay_l[dy].astype(F32)).astype(BF16)
            self.ends[dy, 1, 0] = send(mine, self.end_l.at[dy, pl.ds(0, half)], right)

        def relay_left(self, dy):
            self.relays[dy][1].wait_recv()
            mine = self.at(dy, 3, half, half)
            mine[...] = (mine[...].astype(F32) + self.relay_r[dy].astype(F32)).astype(BF16)
            self.ends[dy, 3, 1] = send(mine, self.end_r.at[dy, pl.ds(half, half)], left_chip)

        def x_sum(self, dy):
            for place in ((1, 0), (1, 1), (3, 0), (3, 1)):
                self.ends[(dy,) + place].wait_recv()
            return self.at(dy, 0)[...].astype(F32) + self.end_l[dy].astype(F32) + self.end_r[dy].astype(F32)

        def send_y(self, dx):
            self.over_y[dx] = send(self.at(1, dx), self.box_y.at[dx], across)

        def add_y(self, dx):
            self.over_y[dx].wait_recv()
            mine = self.at(0, dx)
            mine[...] = (mine[...].astype(F32) + self.box_y[dx].astype(F32)).astype(BF16)

        def end_y(self):
            self.at(1, 0)[...] = self.x_sum(1).astype(BF16)
            self.over_y[0] = send(self.at(1, 0), self.box_y, across)

        def total(self):
            value = self.x_sum(0)
            if self.x_first:
                self.over_y[0].wait_recv()
                value = value + self.box_y[...].astype(F32)
            return value

    sets, parts = {}, {"w": part_w, "f": part_f}
    for number, (name, (part, start, count, x_first)) in enumerate(SETS.items()):
        sets[name] = Columns(parts[part], start, count, x_first, boxes[5 * number:5 * number + 5])

    def multiply(slot):
        to_sibling[slot].wait_recv()
        left[slot, :, pl.ds(0, tokens)] = grad[:, share_of(slot, core)].T
        left[slot, :, pl.ds(tokens, tokens)] = grad_sib[slot].T
        multiply_cols(slot, 0, FIRST_SENT if slot == 0 else SPLIT)

    def multiply_second(slot):
        multiply_cols(slot, FIRST_SENT, SPLIT)

    def multiply_rest(slot):
        multiply_cols(slot, SPLIT, units)

    def multiply_cols(slot, start, end):
        def product(tile):
            part_w[slot, :, tile] = jnp.dot(left[slot], act[:, tile], preferred_element_type=F32).astype(BF16)

        full = (end - start) // TILE

        @pl.loop(0, full)
        def _(n):
            product(pl.ds(pl.multiple_of(start + n * TILE, TILE // 2), TILE))

        if start + full * TILE < end:
            product(pl.ds(start + full * TILE, end - start - full * TILE))

    def multiply_factor(slot):
        if slot == 0:
            cols["sibling"].wait_recv()
        value = jnp.dot(left[slot, :, pl.ds(0, tokens)], cols_own[...], preferred_element_type=F32)
        value = value + jnp.dot(left[slot, :, pl.ds(tokens, tokens)], cols_sib[...], preferred_element_type=F32)
        part_f[slot] = value.astype(BF16)

    def multiply_hidden(first, last):
        @pl.loop(first, last)
        def _(n):
            w_tile(n).wait()
            tile = pl.ds(pl.multiple_of(n * TILE, TILE), TILE)
            hidden[:, tile] = jnp.dot(grad[...], w[n % 2], preferred_element_type=F32).astype(BF16)

            @pl.when(n + 2 < units // TILE)
            def _():
                w_tile(n + 2).start()

        if last == units // TILE:
            results.append(move(hidden, hidden_out))

    def send_x(name, slot):
        dy, dx = ORDER[slot]
        (None, sets[name].near_right, sets[name].far, sets[name].near_left)[dx](dy)

    def relay_x(name, slot):
        dy, dx = ORDER[slot]
        (None, sets[name].relay_right, None, sets[name].relay_left)[dx](dy)

    scale = 1.0 / math.sqrt(tokens * 16)

    def finish(name):
        if SETS[name][0] == "f":
            factor[:, sets[name].cols] = sets[name].total() / (tokens * 16)
            results.append(move(factor.at[:, sets[name].cols], factor_out.at[:, sets[name].cols]))
        else:
            wgrad[:, sets[name].cols] = (sets[name].total() * scale).astype(BF16)
            results.append(move(wgrad.at[:, sets[name].cols], wgrad_out.at[:, sets[name].cols]))

    gather_y(0)
    gather_own(0)
    act_there = send(own_act, act.at[pl.ds(tokens, tokens)], sibling)
    for slot in range(1, CHIPS):
        gather_y(slot)
    own_here.wait()
    for n in range(2):
        w_tile(n).start()
    steps = {
        "yw": wait_y, "own": gather_own, "z": gather_z, "sib": gather_sibling, "cols": cols_z, "colsib": cols_sibling,
        "fwd": forward_z, "mul": multiply, "mulb": multiply_second, "mulv": multiply_rest, "fac": multiply_factor, "x": send_x, "relay": relay_x,
        "y": lambda name, dx: sets[name].send_y(dx), "addy": lambda name, dx: sets[name].add_y(dx),
        "endy": lambda name: sets[name].end_y(), "hid": multiply_hidden, "fin": finish,
    }
    first = True
    drained = 0
    for step, (name, *where) in enumerate(PLAN):
        if name == "mul" and first:
            act_here.wait()
            act_there.wait_recv()
            first = False
        steps[name](*where)
        if name in ("hid", "endy", "fin") and step > len(PLAN) // 2:
            upto = max(drained, len(remotes) - 20)
            for copy in remotes[drained:upto]:
                copy.wait_send()
            drained = upto
    for copy in remotes[drained:]:
        copy.wait_send()
    for copy in results:
        copy.wait()


def shards(out_grad, hidden_act, w_down):
    rows, width = out_grad.shape
    tokens, units = hidden_act.shape
    chunk = width // CHIPS
    share, half = chunk // 2, chunk // 4

    def boxes(count, x_first):
        ways = 2 if x_first else 1
        relay, end = pltpu.VMEM((ways, half, count), BF16), pltpu.VMEM((ways, share, count), BF16)
        over = pltpu.VMEM((share, count) if x_first else (4, share, count), BF16)
        return [relay, relay, end, end, over]

    def body(*refs):
        kernel(*refs[:18], refs[18:-4], *refs[-4:])

    return publish(*pl.pallas_call(
        body,
        out_shape=(
            jax.ShapeDtypeStruct((tokens, units), BF16),
            jax.ShapeDtypeStruct((share, units), BF16),
            jax.ShapeDtypeStruct((share, chunk), F32),
        ),
        in_specs=[pl.BlockSpec(memory_space=pl.ANY)] * 3,
        out_specs=(pl.BlockSpec(memory_space=pl.ANY),) * 3,
        scratch_shapes=[
            pltpu.VMEM((tokens, width), BF16),
            pltpu.VMEM((CHIPS, tokens, share), BF16),
            pltpu.VMEM((tokens, chunk), BF16),
            pltpu.VMEM((tokens, chunk), BF16),
            pltpu.VMEM((2 * tokens, units), BF16),
            pltpu.VMEM((2, width, TILE), BF16),
            pltpu.VMEM((CHIPS, share, 2 * tokens), BF16),
            pltpu.VMEM((CHIPS, share, units), BF16),
            pltpu.VMEM((CHIPS, share, chunk), BF16),
            pltpu.VMEM((tokens, units), BF16),
            pltpu.VMEM((share, units), BF16),
            pltpu.VMEM((share, chunk), F32),
            *[box for _, _, count, x_first in SETS.values() for box in boxes(count, x_first)],
            pltpu.SemaphoreType.DMA((COPIES,)),
            pltpu.SemaphoreType.DMA((COPIES,)),
            pltpu.SemaphoreType.DMA((16,)),
            pltpu.SemaphoreType.DMA((2,)),
        ],
        compiler_params=pltpu.CompilerParams(
            collective_id=0, has_side_effects=True, vmem_limit_bytes=50 * 2**20),
    )(out_grad, hidden_act, w_down))


def publish(hidden, wgrad, factor):
    def body(*refs):
        sems = refs[6]
        copies = [pltpu.make_async_copy(refs[i], refs[3 + i], sems.at[i]) for i in range(3)]
        for copy in copies:
            copy.start()
        for copy in copies:
            copy.wait()

    return pl.pallas_call(
        body,
        out_shape=tuple(jax.ShapeDtypeStruct(a.shape, a.dtype) for a in (hidden, wgrad, factor)),
        in_specs=[pl.BlockSpec(memory_space=pl.ANY)] * 3,
        out_specs=(pl.BlockSpec(memory_space=pl.ANY),) * 3,
        scratch_shapes=[pltpu.SemaphoreType.DMA((3,))],
        compiler_params=pltpu.CompilerParams(vmem_limit_bytes=2**20),
    )(hidden, wgrad, factor)


def solution(mesh):
    return jax.shard_map(
        shards,
        mesh=mesh,
        in_specs=(P(("dp", "tensor"), None), P("dp", "tensor"), P(None, "tensor")),
        out_specs=(P("dp", "tensor"), P("dp", "tensor"), P("dp", "tensor")),
        check_vma=False,
    )
```
